32 devices in a mesh: parts: 2 (over y), blk: 8 (over z, x), gshard: 2 (over core).
Axes of the slice: x: 2, y: 2, z: 4, core: 2. Of those that a mesh axis runs over, the one named last changes fastest.
Arguments:
- screened: bfloat16 [4, 16384, 16384], P('parts', ('blk', 'gshard')), parts along dimension 0, may hold values from -0.046875 to 0.046875
- pairs: bfloat16 [64, 16, 16384], P('parts', None, ('blk', 'gshard')), parts along dimension 0, may hold values from -0.625 to 0.625
- energies: float32 [32], P('parts'), parts along dimension 0, may hold values from -1.5 to 1.5
- nodes: float32 [4], P('parts'), parts along dimension 0, may hold values from 0.2 to 2
- qweights: float32 [4], P('parts'), parts along dimension 0, may hold values from 0.5 to 2
Outputs:
- sigma: float32 [4, 1024], P('parts', ('blk', 'gshard')), parts along dimension 0
The draws below stay inside these ranges and needn't reach their ends.
There are 2 independent parts, one for each index of `parts`. The reference program is written for one: setup_inputs(seed, part) draws one part's arguments, and reference() takes and returns one part's arrays. A program takes and returns all parts, laid end to end along the dimension named above; each array names one. Nothing has to cross between parts.
All inputs are finite; a program needn't handle non-finite values.
Results may differ from the reference program's by a relative error of at most 0.0029.
Values may be sent and summed in bfloat16 or wider, within the bound.
A program may use at most 192 MiB of HBM per device.

```python
import math
import jax
import jax.numpy as jnp
from jax import lax

NG = 16384
NT = 32
KS = 16
F = 2


def level_of(rng, dims, pieces, least, top_value):
    def one(dim, parts):
        steps = jax.random.uniform(jax.random.fold_in(jax.random.fold_in(rng, 6), dim), (parts,), jnp.float32, least / len(pieces), top_value / len(pieces))
        return jnp.repeat(jnp.exp(steps), dims[dim] // parts).reshape((-1,) + (1,) * (len(dims) - dim - 1))

    gain = one(*pieces[0])
    for cut in pieces[1:]:
        gain = gain * one(*cut)
    return gain


def bell_draw(own_key, shape, deviation, bound, cuts=(), dtype=jnp.bfloat16):
    factor_of = level_of(own_key, shape, cuts, -0.22, 0.18) if cuts else 1.0
    entries = jax.random.normal(own_key, shape, jnp.float32) * deviation * factor_of
    return jnp.minimum(jnp.maximum(entries, -bound), bound).astype(dtype)


def setup_inputs(seed: int = 0, part: int = 0) -> dict:
    arg_keys = jax.random.split(jax.random.key(seed), 6)
    own_keys = jax.random.split(jax.random.fold_in(arg_keys[5], part), 6)
    return {
        "screened": bell_draw(own_keys[0], (F, NG, NG), NG ** -0.5, 0.046875, ((1, 16),)),
        "pairs": bell_draw(own_keys[1], (NT, KS, NG), ((NG * KS) ** -0.25), 0.625, ((2, 16),)),
        "energies": jnp.clip(jax.random.uniform(own_keys[2], (KS,), jnp.float32, -1.5, 1.5), -1.5, 1.5),
        "nodes": jnp.clip(jnp.exp(jax.random.uniform(own_keys[3], (F,), jnp.float32, math.log(0.2), math.log(2.0))), 0.2, 2.0),
        "qweights": jnp.clip(jnp.exp(jax.random.uniform(own_keys[4], (F,), jnp.float32, math.log(0.5), math.log(2.0))), 0.5, 2.0),
    }


def reference(screened, pairs, energies, nodes, qweights):
    coupling = qweights[:, None] * energies[None, :] / (energies[None, :] ** 2 + nodes[:, None] ** 2)
    flat = pairs.reshape(NT * KS, NG)
    wide_pairs = pairs.astype(jnp.float32)

    def one_node(items):
        matrix, weights = items
        product = jnp.dot(matrix, flat.T, preferred_element_type=jnp.float32)
        scaled = (product.reshape(NG, NT, KS) * weights[None, None, :]).astype(jnp.bfloat16)
        result = jnp.einsum("nkg,gmk->nm", wide_pairs, scaled.astype(jnp.float32))
        return result.reshape(NT * NT)

    return lax.map(one_node, (screened, coupling))
```

```python
import functools

import jax
import jax.numpy as jnp
from jax import lax
from jax.experimental import pallas as pl
from jax.experimental.pallas import tpu as pltpu
from jax.sharding import PartitionSpec as P

MESH = pl.DeviceIdType.MESH
SLOTS = 3


def grid_of(chips):
    across = 1
    while chips % (2 * across) == 0 and 2 * (2 * across) ** 2 <= chips:
        across *= 2
    return chips // across, across


def place_of(chip, deep, across):
    z, x = lax.div(chip, across), lax.rem(chip, across)
    row = deep - 1 - z
    column = jnp.where(lax.rem(row, 2) == 0, x - 1, across - 1 - x)
    return jnp.where(x == 0, z, deep + row * (across - 1) + column)


def chip_of(place, deep, across):
    if across == 1:
        return place
    past = jnp.maximum(place - deep, 0)
    row, column = lax.div(past, across - 1), lax.rem(past, across - 1)
    x = jnp.where(lax.rem(row, 2) == 0, 1 + column, across - 1 - column)
    return jnp.where(place < deep, place * across, (deep - 1 - row) * across + x)


def kernel(chips, targets, summed, w_hbm, own, energies, nodes, qweights, out, buf, sib_own, w_buf, acc, coup, red_send,
           red_recv, w_sem, send_sem, recv_sem, pass_sem, sib_sem, red_ssem, red_rsem):
    count, rows = w_buf.shape[1], w_buf.shape[2]
    half = buf.shape[2]
    steps = buf.shape[1]
    devices = 2 * chips
    share = red_recv.shape[1]
    group = max(1, devices // targets)
    deep, across = grid_of(chips)
    blk, core = lax.axis_index("blk"), lax.axis_index("gshard")
    me = blk * 2 + core
    other = 1 - core
    place = place_of(blk, deep, across)
    right = chip_of(lax.rem(place + 1, chips), deep, across)
    left = chip_of(lax.rem(place + chips - 1, chips), deep, across)

    def column_block(s):
        u = jnp.maximum(s - 2, 0)
        t, i = lax.div(u, 4), lax.rem(u, 4)
        distance = lax.div(t, 2) + 1
        spot = jnp.where(lax.rem(i, 2) == 0, place + chips - distance, place + distance)
        chip = chip_of(lax.rem(spot, chips), deep, across)
        holder = jnp.where(i < 2, core, other)
        block = chip * 2 + holder
        return jnp.where(s == 0, me, jnp.where(s == 1, blk * 2 + other, block))

    def w_copy(s):
        slot = lax.rem(s, SLOTS)
        start = pl.multiple_of(column_block(s) * rows, rows)
        return pltpu.make_async_copy(w_hbm.at[:, :, pl.ds(start, rows)], w_buf.at[slot], w_sem.at[slot])

    total = 2 + 4 * steps
    for s in range(SLOTS - 1):
        w_copy(jnp.int32(s)).start()

    barrier = pltpu.get_barrier_semaphore()

    def device(j):
        return {"blk": lax.div(j, 2), "gshard": lax.rem(j, 2)}

    def greet(o, carry):
        pl.semaphore_signal(barrier, inc=1, device_id=device(lax.rem(me + o, devices)), device_id_type=MESH)
        return carry

    lax.fori_loop(1, devices, greet, 0)
    pl.semaphore_wait(barrier, devices - 1)

    def ring_copy(src, way, t):
        return pltpu.make_async_remote_copy(
            src_ref=src, dst_ref=buf.at[way, t], send_sem=send_sem.at[way, t], recv_sem=recv_sem.at[way, t],
            device_id={"blk": right if way == 0 else left, "gshard": core}, device_id_type=MESH)

    def pass_copy(way, t):
        return pltpu.make_async_remote_copy(
            src_ref=buf.at[way, t], dst_ref=buf.at[2 + way, t], send_sem=pass_sem.at[way, t],
            recv_sem=recv_sem.at[2 + way, t], device_id={"blk": blk, "gshard": other}, device_id_type=MESH)

    for t in range(min(2, steps)):
        for way in range(2):
            h = t if way == 0 else 1 - t
            ring_copy(own.at[pl.ds(h * half, half)], way, t).start()
    sib_copy = pltpu.make_async_remote_copy(
        src_ref=own, dst_ref=sib_own, send_sem=sib_sem.at[0], recv_sem=sib_sem.at[1],
        device_id={"blk": blk, "gshard": other}, device_id_type=MESH)
    sib_copy.start()

    lane = lax.broadcasted_iota(jnp.int32, (1, half), 1)
    lane_k = lax.rem(lane, summed)
    e_row = jnp.zeros((1, half), jnp.float32)
    for k in range(summed):
        e_row = jnp.where(lane_k == k, energies[k], e_row)
    for f in range(count):
        coup[f] = qweights[f] * e_row / (e_row * e_row + nodes[f] * nodes[f])

    def product(slot, f, piece):
        return lax.dot_general(w_buf[slot, f], piece, (((1,), (1,)), ((), ())), preferred_element_type=jnp.float32)

    def next_w(s):
        @pl.when(s + SLOTS - 1 < total)
        def _():
            w_copy(s + SLOTS - 1).start()

    next_w(jnp.int32(0))
    w_copy(jnp.int32(0)).wait()

    def first(v, carry):
        h, f = lax.div(v, count), lax.rem(v, count)
        acc[h, f] = product(0, f, own[pl.ds(pl.multiple_of(h * half, half), half), :])
        return carry

    lax.fori_loop(0, 2 * count, first, 0)
    next_w(jnp.int32(1))
    w_copy(jnp.int32(1)).wait()
    sib_copy.wait_recv()

    def second(v, carry):
        h, f = lax.div(v, count), lax.rem(v, count)
        acc[h, f] += product(1 % SLOTS, f, sib_own[pl.ds(pl.multiple_of(h * half, half), half), :])
        return carry

    lax.fori_loop(0, 2 * count, second, 0)

    def step(t, carry):
        for way in range(2):
            ring_copy(buf.at[way, t], way, t).wait_recv()

            @pl.when(t + 2 < steps)
            def _():
                ring_copy(buf.at[way, t], way, t + 2).start()

            pass_copy(way, t).start()

        def unit(i, carry):
            s = 2 + 4 * t + i
            next_w(s)
            for way in range(2):
                @pl.when(i == 2 + way)
                def _():
                    pass_copy(way, t).wait_recv()
            w_copy(s).wait()
            slot = lax.rem(s, SLOTS)
            h = lax.rem(t + i, 2)

            def node(f, carry):
                acc[h, f] += product(slot, f, buf[i, t])
                return carry

            lax.fori_loop(0, count, node, 0)
            return carry

        lax.fori_loop(0, 4, unit, 0)
        return carry

    lax.fori_loop(0, steps, step, 0)

    pair_rows = own.shape[0]
    row_k = lax.rem(lax.broadcasted_iota(jnp.int32, (pair_rows, half), 0), summed)
    same = row_k == lax.rem(lax.broadcasted_iota(jnp.int32, (pair_rows, half), 1), summed)
    for f in range(count):
        for h in range(2):
            scaled = (acc[h, f] * coup[f]).astype(jnp.bfloat16)
            part = jnp.dot(own[...], scaled, preferred_element_type=jnp.float32)
            kept = jnp.where(same, part, 0.0).reshape(targets, summed, half).sum(axis=1)
            for n in range(targets):
                red_send[n, pl.ds(f, 1), pl.ds(h * half, half)] = kept[n:n + 1, :]

    def red_copy(j):
        return pltpu.make_async_remote_copy(
            src_ref=red_send.at[pl.ds(lax.div(j, group) * share, share)], dst_ref=red_recv.at[me],
            send_sem=red_ssem.at[j], recv_sem=red_rsem.at[me], device_id=device(j), device_id_type=MESH)

    def send(o, carry):
        red_copy(lax.rem(me + o, devices)).start()
        return carry

    lax.fori_loop(1, devices, send, 0)

    def arrive(o, so_far):
        j = lax.rem(me + o, devices)
        pltpu.make_async_remote_copy(
            src_ref=red_send.at[pl.ds(0, share)], dst_ref=red_recv.at[j], send_sem=red_ssem.at[j],
            recv_sem=red_rsem.at[j], device_id=device(j), device_id_type=MESH).wait_recv()
        return so_far + red_recv[j]

    out[...] = lax.fori_loop(1, devices, arrive, red_send[pl.ds(lax.div(me, group) * share, share)])

    def sent(o, carry):
        red_copy(lax.rem(me + o, devices)).wait_send()
        return carry

    lax.fori_loop(1, devices, sent, 0)
    sib_copy.wait_send()

    def drained(t, carry):
        for way in range(2):
            ring_copy(buf.at[way, 0], way, t).wait_send()
            pass_copy(way, t).wait_send()
        return carry

    lax.fori_loop(0, steps, drained, 0)


def local(chips, screened, pairs, energies, nodes, qweights):
    count, rows, plane_total = screened.shape
    targets, summed, _ = pairs.shape
    pair_rows = targets * summed
    half = pair_rows // 2
    steps = chips - 1
    devices = 2 * chips
    share = max(1, targets // devices)
    smem = pl.BlockSpec(memory_space=pltpu.SMEM)
    vmem = pl.BlockSpec(memory_space=pltpu.VMEM)
    dma = pltpu.SemaphoreType.DMA
    grouped = pl.pallas_call(
        functools.partial(kernel, chips, targets, summed),
        out_shape=jax.ShapeDtypeStruct((share, count, pair_rows), jnp.float32),
        in_specs=[pl.BlockSpec(memory_space=pl.ANY), vmem, smem, smem, smem],
        out_specs=vmem,
        scratch_shapes=[
            pltpu.VMEM((4, steps, half, rows), jnp.bfloat16),
            pltpu.VMEM((pair_rows, rows), jnp.bfloat16),
            pltpu.VMEM((SLOTS, count, rows, rows), jnp.bfloat16),
            pltpu.VMEM((2, count, rows, half), jnp.float32),
            pltpu.VMEM((count, 1, half), jnp.float32),
            pltpu.VMEM((targets, count, pair_rows), jnp.float32),
            pltpu.VMEM((devices, share, count, pair_rows), jnp.float32),
            dma((SLOTS,)),
            dma((2, steps)),
            dma((4, steps)),
            dma((2, steps)),
            dma((2,)),
            dma((devices,)),
            dma((devices,)),
        ],
        compiler_params=pltpu.CompilerParams(
            collective_id=0, has_side_effects=True, vmem_limit_bytes=56 * 1024 * 1024
        ),
        cost_estimate=pl.CostEstimate(
            flops=2 * count * rows * plane_total * pair_rows,
            bytes_accessed=4 * count * rows * plane_total,
            transcendentals=0,
        ),
    )(screened, pairs.reshape(pair_rows, rows), energies, nodes, qweights)
    sigma = grouped.reshape(share, count, targets, summed).sum(axis=3)
    sigma = sigma.transpose(1, 0, 2).reshape(count, share * targets)
    width = targets * targets // devices
    if width < share * targets:
        me = lax.axis_index("blk") * 2 + lax.axis_index("gshard")
        start = lax.rem(me, (share * targets) // width) * width
        sigma = lax.dynamic_slice_in_dim(sigma, start, width, axis=1)
    return sigma


def solution(mesh):
    placed = (
        P("parts", ("blk", "gshard"), None),
        P("parts", None, ("blk", "gshard")),
        P("parts"),
        P("parts"),
        P("parts"),
    )
    return jax.shard_map(
        functools.partial(local, mesh.shape["blk"]),
        mesh=mesh, in_specs=placed, out_specs=P("parts", ("blk", "gshard")), check_vma=False,
    )
```

```python
import functools

import jax
import jax.numpy as jnp
from jax import lax
from jax.experimental import pallas as pl
from jax.experimental.pallas import tpu as pltpu
from jax.sharding import PartitionSpec as P

MESH = pl.DeviceIdType.MESH
SLOTS = 3


def grid_of(chips):
    across = 1
    while chips % (2 * across) == 0 and 2 * (2 * across) ** 2 <= chips:
        across *= 2
    return chips // across, across


def place_of(chip, deep, across):
    z, x = lax.div(chip, across), lax.rem(chip, across)
    row = deep - 1 - z
    column = jnp.where(lax.rem(row, 2) == 0, x - 1, across - 1 - x)
    return jnp.where(x == 0, z, deep + row * (across - 1) + column)


def chip_of(place, deep, across):
    if across == 1:
        return place
    past = jnp.maximum(place - deep, 0)
    row, column = lax.div(past, across - 1), lax.rem(past, across - 1)
    x = jnp.where(lax.rem(row, 2) == 0, 1 + column, across - 1 - column)
    return jnp.where(place < deep, place * across, (deep - 1 - row) * across + x)


def kernel(chips, targets, summed, w_hbm, own, energies, nodes, qweights, out, buf, sib_own, w_buf, acc, far, parts, coup, red_send,
           red_recv, w_sem, send_sem, recv_sem, pass_sem, sib_sem, red_ssem, red_rsem):
    count, rows = w_buf.shape[1], w_buf.shape[2]
    half = buf.shape[2]
    steps = buf.shape[1]
    devices = 2 * chips
    share = red_recv.shape[1]
    group = max(1, devices // targets)
    deep, across = grid_of(chips)
    blk, core = lax.axis_index("blk"), lax.axis_index("gshard")
    me = blk * 2 + core
    other = 1 - core
    place = place_of(blk, deep, across)
    right = chip_of(lax.rem(place + 1, chips), deep, across)
    left = chip_of(lax.rem(place + chips - 1, chips), deep, across)

    def column_block(s):
        u = jnp.where(s < 4, 4 * (steps - 1) + 2 * jnp.maximum(s - 2, 0), s - 4)
        t, i = lax.div(u, 4), lax.rem(u, 4)
        distance = lax.div(t, 2) + 1
        spot = jnp.where(lax.rem(i, 2) == 0, place + chips - distance, place + distance)
        chip = chip_of(lax.rem(spot, chips), deep, across)
        holder = jnp.where(i < 2, core, other)
        block = chip * 2 + holder
        return jnp.where(s == 0, me, jnp.where(s == 1, blk * 2 + other, block))

    def w_copy(s):
        slot = lax.rem(s, SLOTS)
        start = pl.multiple_of(column_block(s) * rows, rows)
        return pltpu.make_async_copy(w_hbm.at[:, :, pl.ds(start, rows)], w_buf.at[slot], w_sem.at[slot])

    total = 4 + 4 * (steps - 1)
    last = steps - 1
    for s in range(SLOTS - 1):
        w_copy(jnp.int32(s)).start()

    barrier = pltpu.get_barrier_semaphore()

    def device(j):
        return {"blk": lax.div(j, 2), "gshard": lax.rem(j, 2)}

    def greet(o, carry):
        pl.semaphore_signal(barrier, inc=1, device_id=device(lax.rem(me + o, devices)), device_id_type=MESH)
        return carry

    lax.fori_loop(1, devices, greet, 0)
    pl.semaphore_wait(barrier, devices - 1)

    def ring_copy(src, way, t):
        return pltpu.make_async_remote_copy(
            src_ref=src, dst_ref=buf.at[way, t], send_sem=send_sem.at[way, t], recv_sem=recv_sem.at[way, t],
            device_id={"blk": right if way == 0 else left, "gshard": core}, device_id_type=MESH)

    def pass_copy(way, t):
        return pltpu.make_async_remote_copy(
            src_ref=buf.at[way, t], dst_ref=buf.at[2 + way, t], send_sem=pass_sem.at[way, t],
            recv_sem=recv_sem.at[2 + way, t], device_id={"blk": blk, "gshard": other}, device_id_type=MESH)

    for t in range(min(2, steps)):
        for way in range(2):
            h = t if way == 0 else 1 - t
            ring_copy(own.at[pl.ds(h * half, half)], way, t).start()
    sib_copy = pltpu.make_async_remote_copy(
        src_ref=own, dst_ref=sib_own, send_sem=sib_sem.at[0], recv_sem=sib_sem.at[1],
        device_id={"blk": blk, "gshard": other}, device_id_type=MESH)
    sib_copy.start()

    lane = lax.broadcasted_iota(jnp.int32, (1, half), 1)
    lane_k = lax.rem(lane, summed)
    e_row = jnp.zeros((1, half), jnp.float32)
    for k in range(summed):
        e_row = jnp.where(lane_k == k, energies[k], e_row)
    for f in range(count):
        coup[f] = qweights[f] * e_row / (e_row * e_row + nodes[f] * nodes[f])

    def product(slot, f, piece):
        return lax.dot_general(w_buf[slot, f], piece, (((1,), (1,)), ((), ())), preferred_element_type=jnp.float32)

    def next_w(s):
        @pl.when(s + SLOTS - 1 < total)
        def _():
            w_copy(s + SLOTS - 1).start()

    next_w(jnp.int32(0))
    w_copy(jnp.int32(0)).wait()

    def first(v, carry):
        h, f = lax.div(v, count), lax.rem(v, count)
        acc[h, f] = product(0, f, own[pl.ds(pl.multiple_of(h * half, half), half), :])
        return carry

    lax.fori_loop(0, 2 * count, first, 0)
    next_w(jnp.int32(1))
    w_copy(jnp.int32(1)).wait()
    sib_copy.wait_recv()

    def second(v, carry):
        h, f = lax.div(v, count), lax.rem(v, count)
        acc[h, f] += product(1 % SLOTS, f, sib_own[pl.ds(pl.multiple_of(h * half, half), half), :])
        return carry

    lax.fori_loop(0, 2 * count, second, 0)

    def from_rows(side, carry):
        s = 2 + side
        next_w(s)
        w_copy(s).wait()
        slot = lax.rem(s, SLOTS)

        def node(f, carry):
            far[side, f] = jnp.dot(own[...], w_buf[slot, f], preferred_element_type=jnp.float32).astype(jnp.bfloat16)
            return carry

        lax.fori_loop(0, count, node, 0)
        return carry

    lax.fori_loop(0, 2, from_rows, 0)

    def step(t, carry):
        for way in range(2):
            ring_copy(buf.at[way, t], way, t).wait_recv()

            @pl.when(t + 2 < steps)
            def _():
                ring_copy(buf.at[way, t], way, t + 2).start()

            pass_copy(way, t).start()

        def unit(i, carry):
            s = 4 + 4 * t + i
            next_w(s)
            for way in range(2):
                @pl.when(i == 2 + way)
                def _():
                    pass_copy(way, t).wait_recv()
            w_copy(s).wait()
            slot = lax.rem(s, SLOTS)
            h = lax.rem(t + i, 2)

            def node(f, carry):
                acc[h, f] += product(slot, f, buf[i, t])
                return carry

            lax.fori_loop(0, count, node, 0)
            return carry

        lax.fori_loop(0, 4, unit, 0)
        return carry

    lax.fori_loop(0, last, step, 0)

    for f in range(count):
        for h in range(2):
            scaled = (acc[h, f] * coup[f]).astype(jnp.bfloat16)
            parts[h, f] = jnp.dot(own[...], scaled, preferred_element_type=jnp.float32)

    def met(side, f, h):
        return coup[f] * lax.dot_general(
            far[side, f], buf[2 * side + h, last], (((1,), (1,)), ((), ())), preferred_element_type=jnp.float32)

    for way in range(2):
        ring_copy(buf.at[way, last], way, last).wait_recv()
        pass_copy(way, last).start()
    for h in range(2):
        for f in range(count):
            parts[h, f] += met(0, f, h)

    pair_rows = own.shape[0]
    row_k = lax.rem(lax.broadcasted_iota(jnp.int32, (pair_rows, half), 0), summed)
    same = row_k == lax.rem(lax.broadcasted_iota(jnp.int32, (pair_rows, half), 1), summed)
    for h in range(2):
        pass_copy(h, last).wait_recv()
        for f in range(count):
            part = parts[h, f] + met(1, f, h)
            kept = jnp.where(same, part, 0.0).reshape(targets, summed, half).sum(axis=1)
            for n in range(targets):
                red_send[n, pl.ds(f, 1), pl.ds(h * half, half)] = kept[n:n + 1, :]

    def red_copy(j):
        return pltpu.make_async_remote_copy(
            src_ref=red_send.at[pl.ds(lax.div(j, group) * share, share)], dst_ref=red_recv.at[me],
            send_sem=red_ssem.at[j], recv_sem=red_rsem.at[me], device_id=device(j), device_id_type=MESH)

    def send(o, carry):
        red_copy(lax.rem(me + o, devices)).start()
        return carry

    lax.fori_loop(1, devices, send, 0)

    def arrive(o, so_far):
        j = lax.rem(me + o, devices)
        pltpu.make_async_remote_copy(
            src_ref=red_send.at[pl.ds(0, share)], dst_ref=red_recv.at[j], send_sem=red_ssem.at[j],
            recv_sem=red_rsem.at[j], device_id=device(j), device_id_type=MESH).wait_recv()
        return so_far + red_recv[j]

    out[...] = lax.fori_loop(1, devices, arrive, red_send[pl.ds(lax.div(me, group) * share, share)])

    def sent(o, carry):
        red_copy(lax.rem(me + o, devices)).wait_send()
        return carry

    lax.fori_loop(1, devices, sent, 0)
    sib_copy.wait_send()

    def drained(t, carry):
        for way in range(2):
            ring_copy(buf.at[way, 0], way, t).wait_send()
            pass_copy(way, t).wait_send()
        return carry

    lax.fori_loop(0, steps, drained, 0)


def local(chips, screened, pairs, energies, nodes, qweights):
    count, rows, plane_total = screened.shape
    targets, summed, _ = pairs.shape
    pair_rows = targets * summed
    half = pair_rows // 2
    steps = chips - 1
    devices = 2 * chips
    share = max(1, targets // devices)
    smem = pl.BlockSpec(memory_space=pltpu.SMEM)
    vmem = pl.BlockSpec(memory_space=pltpu.VMEM)
    dma = pltpu.SemaphoreType.DMA
    grouped = pl.pallas_call(
        functools.partial(kernel, chips, targets, summed),
        out_shape=jax.ShapeDtypeStruct((share, count, pair_rows), jnp.float32),
        in_specs=[pl.BlockSpec(memory_space=pl.ANY), vmem, smem, smem, smem],
        out_specs=vmem,
        scratch_shapes=[
            pltpu.VMEM((4, steps, half, rows), jnp.bfloat16),
            pltpu.VMEM((pair_rows, rows), jnp.bfloat16),
            pltpu.VMEM((SLOTS, count, rows, rows), jnp.bfloat16),
            pltpu.VMEM((2, count, rows, half), jnp.float32),
            pltpu.VMEM((2, count, pair_rows, rows), jnp.bfloat16),
            pltpu.VMEM((2, count, pair_rows, half), jnp.float32),
            pltpu.VMEM((count, 1, half), jnp.float32),
            pltpu.VMEM((targets, count, pair_rows), jnp.float32),
            pltpu.VMEM((devices, share, count, pair_rows), jnp.float32),
            dma((SLOTS,)),
            dma((2, steps)),
            dma((4, steps)),
            dma((2, steps)),
            dma((2,)),
            dma((devices,)),
            dma((devices,)),
        ],
        compiler_params=pltpu.CompilerParams(
            collective_id=0, has_side_effects=True, vmem_limit_bytes=56 * 1024 * 1024
        ),
        cost_estimate=pl.CostEstimate(
            flops=2 * count * rows * plane_total * pair_rows,
            bytes_accessed=4 * count * rows * plane_total,
            transcendentals=0,
        ),
    )(screened, pairs.reshape(pair_rows, rows), energies, nodes, qweights)
    sigma = grouped.reshape(share, count, targets, summed).sum(axis=3)
    sigma = sigma.transpose(1, 0, 2).reshape(count, share * targets)
    width = targets * targets // devices
    if width < share * targets:
        me = lax.axis_index("blk") * 2 + lax.axis_index("gshard")
        start = lax.rem(me, (share * targets) // width) * width
        sigma = lax.dynamic_slice_in_dim(sigma, start, width, axis=1)
    return sigma


def solution(mesh):
    placed = (
        P("parts", ("blk", "gshard"), None),
        P("parts", None, ("blk", "gshard")),
        P("parts"),
        P("parts"),
        P("parts"),
    )
    return jax.shard_map(
        functools.partial(local, mesh.shape["blk"]),
        mesh=mesh, in_specs=placed, out_specs=P("parts", ("blk", "gshard")), check_vma=False,
    )
```

```python
import functools

import jax
import jax.numpy as jnp
from jax import lax
from jax.experimental import pallas as pl
from jax.experimental.pallas import tpu as pltpu
from jax.sharding import PartitionSpec as P

MESH = pl.DeviceIdType.MESH
SLOTS = 3


def grid_of(chips):
    across = 1
    while chips % (2 * across) == 0 and 2 * (2 * across) ** 2 <= chips:
        across *= 2
    return chips // across, across


def place_of(chip, deep, across):
    z, x = lax.div(chip, across), lax.rem(chip, across)
    row = deep - 1 - z
    column = jnp.where(lax.rem(row, 2) == 0, x - 1, across - 1 - x)
    return jnp.where(x == 0, z, deep + row * (across - 1) + column)


def chip_of(place, deep, across):
    if across == 1:
        return place
    past = jnp.maximum(place - deep, 0)
    row, column = lax.div(past, across - 1), lax.rem(past, across - 1)
    x = jnp.where(lax.rem(row, 2) == 0, 1 + column, across - 1 - column)
    return jnp.where(place < deep, place * across, (deep - 1 - row) * across + x)


def kernel(chips, targets, summed, w_hbm, own, energies, nodes, qweights, out, buf, sib_own, w_buf, acc, far, parts, coup, red_send,
           red_recv, w_sem, cut_send, cut_recv, cut_pass, send_sem, recv_sem, pass_sem, sib_sem, red_ssem, red_rsem):
    count, rows = w_buf.shape[1], w_buf.shape[2]
    half = buf.shape[2]
    steps = buf.shape[1]
    devices = 2 * chips
    share = red_recv.shape[1]
    group = max(1, devices // targets)
    deep, across = grid_of(chips)
    blk, core = lax.axis_index("blk"), lax.axis_index("gshard")
    me = blk * 2 + core
    other = 1 - core
    place = place_of(blk, deep, across)
    right = chip_of(lax.rem(place + 1, chips), deep, across)
    left = chip_of(lax.rem(place + chips - 1, chips), deep, across)

    def column_block(s):
        u = jnp.where(s < 4, 4 * (steps - 1) + 2 * jnp.maximum(s - 2, 0), s - 4)
        t, i = lax.div(u, 4), lax.rem(u, 4)
        distance = lax.div(t, 2) + 1
        spot = jnp.where(lax.rem(i, 2) == 0, place + chips - distance, place + distance)
        chip = chip_of(lax.rem(spot, chips), deep, across)
        holder = jnp.where(i < 2, core, other)
        block = chip * 2 + holder
        return jnp.where(s == 0, me, jnp.where(s == 1, blk * 2 + other, block))

    def w_copy(s):
        slot = lax.rem(s, SLOTS)
        start = pl.multiple_of(column_block(s) * rows, rows)
        return pltpu.make_async_copy(w_hbm.at[:, :, pl.ds(start, rows)], w_buf.at[slot], w_sem.at[slot])

    total = 4 + 4 * (steps - 1)
    last = steps - 1
    for s in range(SLOTS - 1):
        w_copy(jnp.int32(s)).start()

    barrier = pltpu.get_barrier_semaphore()

    def device(j):
        return {"blk": lax.div(j, 2), "gshard": lax.rem(j, 2)}

    for chip, holder in ((left, core), (right, core), (blk, other)):
        pl.semaphore_signal(barrier, inc=1, device_id={"blk": chip, "gshard": holder}, device_id_type=MESH)
    pl.semaphore_wait(barrier, 3)

    def ring_copy(src, way, t):
        return pltpu.make_async_remote_copy(
            src_ref=src, dst_ref=buf.at[way, t], send_sem=send_sem.at[way, t], recv_sem=recv_sem.at[way, t],
            device_id={"blk": right if way == 0 else left, "gshard": core}, device_id_type=MESH)

    def pass_copy(way, t):
        return pltpu.make_async_remote_copy(
            src_ref=buf.at[way, t], dst_ref=buf.at[2 + way, t], send_sem=pass_sem.at[way, t],
            recv_sem=recv_sem.at[2 + way, t], device_id={"blk": blk, "gshard": other}, device_id_type=MESH)

    cuts = cut_send.shape[1]
    width = rows // cuts

    def cut(way, q):
        return buf.at[way, last, :, pl.ds(q * width, width)]

    def cut_copy(way, q):
        return pltpu.make_async_remote_copy(
            src_ref=buf.at[way, last - 2, :, pl.ds(q * width, width)], dst_ref=cut(way, q),
            send_sem=cut_send.at[way, q], recv_sem=cut_recv.at[way, q],
            device_id={"blk": right if way == 0 else left, "gshard": core}, device_id_type=MESH)

    def cut_pass_copy(way, q):
        return pltpu.make_async_remote_copy(
            src_ref=cut(way, q), dst_ref=cut(2 + way, q), send_sem=cut_pass.at[way, q],
            recv_sem=cut_recv.at[2 + way, q], device_id={"blk": blk, "gshard": other}, device_id_type=MESH)

    def own_copy(way, t):
        h = t if way == 0 else 1 - t
        return ring_copy(own.at[pl.ds(h * half, half)], way, t)

    for way in range(2):
        own_copy(way, 0).start()
    sib_copy = pltpu.make_async_remote_copy(
        src_ref=own, dst_ref=sib_own, send_sem=sib_sem.at[0], recv_sem=sib_sem.at[1],
        device_id={"blk": blk, "gshard": other}, device_id_type=MESH)
    sib_copy.start()

    lane = lax.broadcasted_iota(jnp.int32, (1, half), 1)
    lane_k = lax.rem(lane, summed)
    e_row = jnp.zeros((1, half), jnp.float32)
    for k in range(summed):
        e_row = jnp.where(lane_k == k, energies[k], e_row)
    for f in range(count):
        coup[f] = qweights[f] * e_row / (e_row * e_row + nodes[f] * nodes[f])

    def product(slot, f, piece):
        return lax.dot_general(w_buf[slot, f], piece, (((1,), (1,)), ((), ())), preferred_element_type=jnp.float32)

    def next_w(s):
        @pl.when(s + SLOTS - 1 < total)
        def _():
            w_copy(s + SLOTS - 1).start()

    next_w(jnp.int32(0))
    w_copy(jnp.int32(0)).wait()

    def first(v, carry):
        h, f = lax.div(v, count), lax.rem(v, count)
        acc[h, f] = product(0, f, own[pl.ds(pl.multiple_of(h * half, half), half), :])
        return carry

    lax.fori_loop(0, 2 * count, first, 0)
    if steps > 1:
        for way in range(2):
            own_copy(way, 1).start()
    next_w(jnp.int32(1))
    w_copy(jnp.int32(1)).wait()
    sib_copy.wait_recv()

    def second(v, carry):
        h, f = lax.div(v, count), lax.rem(v, count)
        acc[h, f] += product(1 % SLOTS, f, sib_own[pl.ds(pl.multiple_of(h * half, half), half), :])
        return carry

    lax.fori_loop(0, 2 * count, second, 0)

    def from_rows(side, carry):
        s = 2 + side
        next_w(s)
        w_copy(s).wait()
        slot = lax.rem(s, SLOTS)

        def node(f, carry):
            far[side, f] = jnp.dot(own[...], w_buf[slot, f], preferred_element_type=jnp.float32).astype(jnp.bfloat16)
            return carry

        lax.fori_loop(0, count, node, 0)
        return carry

    lax.fori_loop(0, 2, from_rows, 0)

    def step(t, carry):
        for way in range(2):
            ring_copy(buf.at[way, t], way, t).wait_recv()

            @pl.when(t + 2 < last)
            def _():
                ring_copy(buf.at[way, t], way, t + 2).start()

            @pl.when(t + 2 == last)
            def _():
                for q in range(cuts):
                    cut_copy(way, q).start()

            pass_copy(way, t).start()

        def unit(i, carry):
            s = 4 + 4 * t + i
            next_w(s)
            for way in range(2):
                @pl.when(i == 2 + way)
                def _():
                    pass_copy(way, t).wait_recv()
            w_copy(s).wait()
            slot = lax.rem(s, SLOTS)
            h = lax.rem(t + i, 2)

            def node(f, carry):
                acc[h, f] += product(slot, f, buf[i, t])
                return carry

            lax.fori_loop(0, count, node, 0)
            return carry

        lax.fori_loop(0, 4, unit, 0)
        return carry

    lax.fori_loop(0, last, step, 0)

    for f in range(count):
        for h in range(2):
            scaled = (acc[h, f] * coup[f]).astype(jnp.bfloat16)
            parts[h, f] = jnp.dot(own[...], scaled, preferred_element_type=jnp.float32)

    def met(side, f, h, q):
        columns = pl.ds(q * width, width)
        return coup[f] * lax.dot_general(
            far[side, f, :, columns], buf[2 * side + h, last, :, columns], (((1,), (1,)), ((), ())),
            preferred_element_type=jnp.float32)

    for q in range(cuts):
        for way in range(2):
            cut_copy(way, q).wait_recv()
            cut_pass_copy(way, q).start()
        for h in range(2):
            for f in range(count):
                parts[h, f] += met(0, f, h, q)
        if q < cuts - 1:
            for h in range(2):
                cut_pass_copy(h, q).wait_recv()
                for f in range(count):
                    parts[h, f] += met(1, f, h, q)

    pair_rows = own.shape[0]
    row_k = lax.rem(lax.broadcasted_iota(jnp.int32, (pair_rows, half), 0), summed)
    same = row_k == lax.rem(lax.broadcasted_iota(jnp.int32, (pair_rows, half), 1), summed)
    for h in range(2):
        cut_pass_copy(h, cuts - 1).wait_recv()
        for f in range(count):
            part = parts[h, f] + met(1, f, h, cuts - 1)
            kept = jnp.where(same, part, 0.0).reshape(targets, summed, half).sum(axis=1)
            for n in range(targets):
                red_send[n, pl.ds(f, 1), pl.ds(h * half, half)] = kept[n:n + 1, :]

    def red_copy(j):
        return pltpu.make_async_remote_copy(
            src_ref=red_send.at[pl.ds(lax.div(j, group) * share, share)], dst_ref=red_recv.at[me],
            send_sem=red_ssem.at[j], recv_sem=red_rsem.at[me], device_id=device(j), device_id_type=MESH)

    def send(o, carry):
        red_copy(lax.rem(me + o, devices)).start()
        return carry

    lax.fori_loop(1, devices, send, 0)

    def arrive(o, so_far):
        j = lax.rem(me + o, devices)
        pltpu.make_async_remote_copy(
            src_ref=red_send.at[pl.ds(0, share)], dst_ref=red_recv.at[j], send_sem=red_ssem.at[j],
            recv_sem=red_rsem.at[j], device_id=device(j), device_id_type=MESH).wait_recv()
        return so_far + red_recv[j]

    sums = lax.fori_loop(1, devices, arrive, red_send[pl.ds(lax.div(me, group) * share, share)])
    pick = jnp.where(
        lax.div(lax.broadcasted_iota(jnp.int32, (pair_rows, targets), 0), summed)
        == lax.broadcasted_iota(jnp.int32, (pair_rows, targets), 1), 1.0, 0.0)
    for n in range(share):
        out[:, pl.ds(n * targets, targets)] = jnp.dot(
            sums[n], pick, precision=lax.Precision.HIGHEST, preferred_element_type=jnp.float32)

    def sent(o, carry):
        red_copy(lax.rem(me + o, devices)).wait_send()
        return carry

    lax.fori_loop(1, devices, sent, 0)
    sib_copy.wait_send()

    def drained(t, carry):
        for way in range(2):
            ring_copy(buf.at[way, 0], way, t).wait_send()
            pass_copy(way, t).wait_send()
        return carry

    lax.fori_loop(0, last, drained, 0)
    for q in range(cuts):
        for way in range(2):
            cut_copy(way, q).wait_send()
            cut_pass_copy(way, q).wait_send()


def local(chips, screened, pairs, energies, nodes, qweights):
    count, rows, plane_total = screened.shape
    targets, summed, _ = pairs.shape
    pair_rows = targets * summed
    half = pair_rows // 2
    steps = chips - 1
    devices = 2 * chips
    share = max(1, targets // devices)
    cuts = max(1, rows // 256)
    smem = pl.BlockSpec(memory_space=pltpu.SMEM)
    vmem = pl.BlockSpec(memory_space=pltpu.VMEM)
    dma = pltpu.SemaphoreType.DMA
    sigma = pl.pallas_call(
        functools.partial(kernel, chips, targets, summed),
        out_shape=jax.ShapeDtypeStruct((count, share * targets), jnp.float32),
        in_specs=[pl.BlockSpec(memory_space=pl.ANY), vmem, smem, smem, smem],
        out_specs=vmem,
        scratch_shapes=[
            pltpu.VMEM((4, steps, half, rows), jnp.bfloat16),
            pltpu.VMEM((pair_rows, rows), jnp.bfloat16),
            pltpu.VMEM((SLOTS, count, rows, rows), jnp.bfloat16),
            pltpu.VMEM((2, count, rows, half), jnp.float32),
            pltpu.VMEM((2, count, pair_rows, rows), jnp.bfloat16),
            pltpu.VMEM((2, count, pair_rows, half), jnp.float32),
            pltpu.VMEM((count, 1, half), jnp.float32),
            pltpu.VMEM((targets, count, pair_rows), jnp.float32),
            pltpu.VMEM((devices, share, count, pair_rows), jnp.float32),
            dma((SLOTS,)),
            dma((2, cuts)),
            dma((4, cuts)),
            dma((2, cuts)),
            dma((2, steps)),
            dma((4, steps)),
            dma((2, steps)),
            dma((2,)),
            dma((devices,)),
            dma((devices,)),
        ],
        compiler_params=pltpu.CompilerParams(
            collective_id=0, has_side_effects=True, vmem_limit_bytes=56 * 1024 * 1024
        ),
        cost_estimate=pl.CostEstimate(
            flops=2 * count * rows * plane_total * pair_rows,
            bytes_accessed=4 * count * rows * plane_total,
            transcendentals=0,
        ),
    )(screened, pairs.reshape(pair_rows, rows), energies, nodes, qweights)
    width = targets * targets // devices
    if width < share * targets:
        me = lax.axis_index("blk") * 2 + lax.axis_index("gshard")
        start = lax.rem(me, (share * targets) // width) * width
        sigma = lax.dynamic_slice_in_dim(sigma, start, width, axis=1)
    return sigma


def solution(mesh):
    placed = (
        P("parts", ("blk", "gshard"), None),
        P("parts", None, ("blk", "gshard")),
        P("parts"),
        P("parts"),
        P("parts"),
    )
    return jax.shard_map(
        functools.partial(local, mesh.shape["blk"]),
        mesh=mesh, in_specs=placed, out_specs=P("parts", ("blk", "gshard")), check_vma=False,
    )
```
